512 devices in a mesh: pipe: 8 (over x, core), blk: 32 (over z, y_hi), uly: 2 (over y_lo).
Axes of the slice: x: 4, y: 4 (y_hi: 2, y_lo: 2; y = y_hi * 2 + y_lo), z: 16, core: 2. Of those that a mesh axis runs over, the one named last changes fastest.
Arguments:
- slot_order: int32 [64], replicated, may hold values from 0 to 63, each once
- query_fwd: bfloat16 [8, 4096, 4096], P('pipe', ('blk', 'uly')), may hold values from -5 to 5
- key_fwd: bfloat16 [8, 4096, 512], P('pipe', ('blk', 'uly')), may hold values from -5 to 5
- value_forward: bfloat16 [8, 4096, 512], P('pipe', ('blk', 'uly')), may hold values from -6 to 6
- query_bwd: bfloat16 [8, 4096, 4096], P('pipe', ('blk', 'uly')), may hold values from -5 to 5
- key_bwd: bfloat16 [8, 4096, 512], P('pipe', ('blk', 'uly')), may hold values from -5 to 5
- value_backward: bfloat16 [8, 4096, 512], P('pipe', ('blk', 'uly')), may hold values from -6 to 6
- out_grad: bfloat16 [8, 4096, 4096], P('pipe', ('blk', 'uly')), may hold values from -6 to 6
Outputs:
- handed: bfloat16 [8, 4096, 4096], P('pipe', ('blk', 'uly'))
- query_grad: bfloat16 [8, 4096, 4096], P('pipe', ('blk', 'uly'))
- key_grad: bfloat16 [8, 4096, 512], P('pipe', ('blk', 'uly'))
- value_grad: bfloat16 [8, 4096, 512], P('pipe', ('blk', 'uly'))
The draws below stay inside these ranges and needn't reach their ends.
Inputs may be any that keep to these rules, and one draw needn't show every extreme that they name: `slot_order`: each slot holds a different part.
All inputs are finite; a program needn't handle non-finite values.
Results may differ from the reference program's by a relative error of at most 0.011.
Values may be sent and summed in bfloat16 or wider, within the bound.
A program may use at most 128 MiB of HBM per device.

```python
import jax
import jax.numpy as jnp
from jax import lax

HQ = 32
KEY_HEADS = 4
HEAD_SIZE = 128
TOK_DEV = 64
VISIBLE_GROUPS = 4
QUERY_PER_KEY = 8
GROUP_TOKENS = 128
QUERY_GROUPS = 32
SLOTS = 64
SEQUENCE_TOKENS = 4096
N_PIPE = 8


def draw_query_fwd(key, part):
    key = jax.random.fold_in(key, 1)
    every_dimension = (N_PIPE, SEQUENCE_TOKENS, KEY_HEADS, QUERY_PER_KEY, HEAD_SIZE)
    base_random_field = jnp.clip(jax.random.normal(key, every_dimension), -4.0, 4.0)
    return base_random_field.reshape(N_PIPE, SEQUENCE_TOKENS, HQ * HEAD_SIZE).astype(jnp.bfloat16)


def draw_query_bwd(key, part):
    key = jax.random.fold_in(key, 2)
    every_dimension = (N_PIPE, SEQUENCE_TOKENS, KEY_HEADS, QUERY_PER_KEY, HEAD_SIZE)
    base_random_field = jnp.clip(jax.random.normal(key, every_dimension), -4.0, 4.0)
    return base_random_field.reshape(N_PIPE, SEQUENCE_TOKENS, HQ * HEAD_SIZE).astype(jnp.bfloat16)


def draw_key_fwd(key, part):
    key = jax.random.fold_in(key, 3)
    every_dimension = (N_PIPE, SEQUENCE_TOKENS, KEY_HEADS, HEAD_SIZE)
    base_random_field = jnp.clip(jax.random.normal(key, every_dimension), -4.0, 4.0)
    return base_random_field.reshape(N_PIPE, SEQUENCE_TOKENS, KEY_HEADS * HEAD_SIZE).astype(jnp.bfloat16)


def draw_key_bwd(key, part):
    key = jax.random.fold_in(key, 4)
    every_dimension = (N_PIPE, SEQUENCE_TOKENS, KEY_HEADS, HEAD_SIZE)
    base_random_field = jnp.clip(jax.random.normal(key, every_dimension), -4.0, 4.0)
    return base_random_field.reshape(N_PIPE, SEQUENCE_TOKENS, KEY_HEADS * HEAD_SIZE).astype(jnp.bfloat16)


def levels(own_key, dims, cuts, least, largest):
    loudness = 1.0
    for position, parts in cuts:
        draws = jax.random.uniform(jax.random.fold_in(jax.random.fold_in(own_key, 6), position), (parts,), jnp.float32, least / len(cuts), largest / len(cuts))
        loudness = loudness * jnp.repeat(jnp.exp(draws), dims[position] // parts).reshape((-1,) + (1,) * (len(dims) - 1 - position))
    return loudness


def scatter_about(key, shape, deviation, bound, cuts=(), kind=jnp.bfloat16):
    loudness = levels(key, shape, cuts, -0.22, 0.18) if cuts else 1.0
    drawn = jax.random.normal(key, shape, jnp.float32) * deviation * loudness
    return jnp.minimum(jnp.maximum(drawn, -bound), bound).astype(kind)


def setup_inputs(seed: int = 0) -> dict:
    keys = jax.random.split(jax.random.key(seed), 9)
    slot_order = jax.random.permutation(keys[0], SLOTS).astype(jnp.int32)
    query_fwd = draw_query_fwd(jax.random.fold_in(keys[8], 71), 0)
    key_fwd = draw_key_fwd(jax.random.fold_in(keys[8], 71), 0)
    value_forward = scatter_about(keys[3], (N_PIPE, SEQUENCE_TOKENS, KEY_HEADS * HEAD_SIZE), 1.0, 6.0, ((0, 8), (1, 64)))
    query_bwd = draw_query_bwd(jax.random.fold_in(keys[8], 71), 0)
    key_bwd = draw_key_bwd(jax.random.fold_in(keys[8], 71), 0)
    value_backward = scatter_about(keys[6], (N_PIPE, SEQUENCE_TOKENS, KEY_HEADS * HEAD_SIZE), 1.0, 6.0, ((0, 8), (1, 64)))
    out_grad = scatter_about(keys[7], (N_PIPE, SEQUENCE_TOKENS, HQ * HEAD_SIZE), 1.0, 6.0, ((0, 8), (1, 64)))
    return dict(slot_order=slot_order, query_fwd=query_fwd, key_fwd=key_fwd, value_forward=value_forward, query_bwd=query_bwd, key_bwd=key_bwd, value_backward=value_backward, out_grad=out_grad)


NEG = -1.0e30


def token_positions(slot_order):
    row_index = jnp.arange(SEQUENCE_TOKENS, dtype=jnp.int32)
    return slot_order[row_index // TOK_DEV].astype(jnp.int32) * TOK_DEV + row_index % TOK_DEV


def window_rows(array, group_id):
    pieces = []
    for cycle_step in range(VISIBLE_GROUPS):
        start = ((group_id - cycle_step + QUERY_GROUPS) % QUERY_GROUPS) * GROUP_TOKENS
        pieces.append(lax.dynamic_slice_in_dim(array, start.astype(jnp.int32), GROUP_TOKENS, 0))
    return jnp.concatenate(pieces, axis=0)


def lowered(array):
    return lax.optimization_barrier(array.astype(jnp.bfloat16)).astype(jnp.float32)


def attend(query_rows, key_row_block, value_row_block, allowed):
    query_head_split = query_rows.reshape(GROUP_TOKENS, KEY_HEADS, QUERY_PER_KEY, HEAD_SIZE).astype(jnp.float32)
    key_head_split = key_row_block.reshape(VISIBLE_GROUPS * GROUP_TOKENS, KEY_HEADS, HEAD_SIZE).astype(jnp.float32)
    raw_scores = jnp.einsum('qgrd,kgd->grqk', query_head_split, key_head_split) * (HEAD_SIZE ** -0.5)
    scores = jnp.where(allowed[None, None], raw_scores, NEG)
    row_peak = jnp.max(scores, axis=-1)
    raised = jnp.exp(scores - row_peak[..., None])
    row_total = jnp.sum(raised, axis=-1)
    value_head_split = value_row_block.reshape(VISIBLE_GROUPS * GROUP_TOKENS, KEY_HEADS, HEAD_SIZE).astype(jnp.float32)
    weighted = jnp.einsum('grqk,kgd->qgrd', lowered(raised), value_head_split)
    weighted = weighted / jnp.transpose(row_total, (2, 0, 1))[..., None]
    return query_head_split, key_head_split, value_head_split, scores, row_peak, row_total, weighted


def group_mask(positions, group_id):
    query_pos = lax.dynamic_slice_in_dim(positions, (group_id * GROUP_TOKENS).astype(jnp.int32), GROUP_TOKENS, 0)
    return query_pos[:, None] >= window_rows(positions, group_id)[None, :]


def forward_section(query_rows, key_row_block, value_row_block, positions):
    def one_group(group_id):
        allowed = group_mask(positions, group_id)
        rows_here = lax.dynamic_slice_in_dim(query_rows, (group_id * GROUP_TOKENS).astype(jnp.int32), GROUP_TOKENS, 0)
        weighted = attend(rows_here, window_rows(key_row_block, group_id), window_rows(value_row_block, group_id), allowed)[6]
        return weighted.reshape(GROUP_TOKENS, HQ * HEAD_SIZE).astype(jnp.bfloat16)

    outputs = lax.map(one_group, jnp.arange(QUERY_GROUPS, dtype=jnp.int32))
    return outputs.reshape(SEQUENCE_TOKENS, HQ * HEAD_SIZE)


def backward_section(query_rows, key_row_block, value_row_block, cotangent, positions):
    def one_group(group_id):
        allowed = group_mask(positions, group_id)
        start = (group_id * GROUP_TOKENS).astype(jnp.int32)
        rows_here = lax.dynamic_slice_in_dim(query_rows, start, GROUP_TOKENS, 0)
        local_gradients = lax.dynamic_slice_in_dim(cotangent, start, GROUP_TOKENS, 0)
        query_head_split, key_head_split, value_head_split, scores, row_peak, row_total, weighted = attend(
            rows_here, window_rows(key_row_block, group_id), window_rows(value_row_block, group_id), allowed)
        log_total = row_peak + jnp.log(row_total)
        gradient_heads = local_gradients.reshape(GROUP_TOKENS, KEY_HEADS, QUERY_PER_KEY, HEAD_SIZE).astype(jnp.float32)
        row_delta = jnp.transpose(jnp.sum(gradient_heads * weighted, axis=-1), (1, 2, 0))
        attn_probs = jnp.exp(scores - log_total[..., None])
        grad_probs = jnp.einsum('qgrd,kgd->grqk', gradient_heads, value_head_split)
        grad_scores = lowered(attn_probs * (grad_probs - row_delta[..., None]))
        inv_root = HEAD_SIZE ** -0.5
        grad_query = jnp.einsum('grqk,kgd->qgrd', grad_scores, key_head_split) * inv_root
        key_gradient = jnp.einsum('grqk,qgrd->kgd', grad_scores, query_head_split) * inv_root
        value_gradient = jnp.einsum('grqk,qgrd->kgd', lowered(attn_probs), gradient_heads)
        return (grad_query.reshape(GROUP_TOKENS, HQ * HEAD_SIZE).astype(jnp.bfloat16),
                key_gradient.reshape(VISIBLE_GROUPS, GROUP_TOKENS, KEY_HEADS * HEAD_SIZE),
                value_gradient.reshape(VISIBLE_GROUPS, GROUP_TOKENS, KEY_HEADS * HEAD_SIZE))

    grad_query, key_gradient, value_gradient = lax.map(one_group, jnp.arange(QUERY_GROUPS, dtype=jnp.int32))
    key_accumulated = jnp.zeros((QUERY_GROUPS, GROUP_TOKENS, KEY_HEADS * HEAD_SIZE), jnp.float32)
    value_accumulated = jnp.zeros((QUERY_GROUPS, GROUP_TOKENS, KEY_HEADS * HEAD_SIZE), jnp.float32)
    for cycle_step in range(VISIBLE_GROUPS):
        key_accumulated = key_accumulated + jnp.roll(key_gradient[:, cycle_step], -cycle_step, axis=0)
        value_accumulated = value_accumulated + jnp.roll(value_gradient[:, cycle_step], -cycle_step, axis=0)
    return (grad_query.reshape(SEQUENCE_TOKENS, HQ * HEAD_SIZE),
            key_accumulated.reshape(SEQUENCE_TOKENS, KEY_HEADS * HEAD_SIZE).astype(jnp.bfloat16),
            value_accumulated.reshape(SEQUENCE_TOKENS, KEY_HEADS * HEAD_SIZE).astype(jnp.bfloat16))


def reference(slot_order, query_fwd, key_fwd, value_forward, query_bwd, key_bwd, value_backward, out_grad):
    positions = token_positions(slot_order)
    attention = lax.map(lambda section_item: forward_section(section_item[0], section_item[1], section_item[2], positions),
                        (query_fwd, key_fwd, value_forward))
    handed = jnp.concatenate([jnp.zeros_like(attention[:1]), attention[:-1]], axis=0)
    query_grad, key_grad, value_grad = lax.map(
        lambda section_item: backward_section(section_item[0], section_item[1], section_item[2], section_item[3], positions),
        (query_bwd, key_bwd, value_backward, out_grad))
    return handed, query_grad, key_grad, value_grad
```

```python
import functools
import math

import jax
import jax.numpy as jnp
from jax import lax
from jax.experimental import pallas as pl
from jax.experimental.pallas import tpu as pltpu
from jax.sharding import PartitionSpec as P

HEAD = 128
GQA = 8
KVH = 4
TOK = 64
SLOTS_SEEN = 8
KEYS = SLOTS_SEEN * TOK
ROWS = GQA * TOK
WIDE = GQA * HEAD
NEG = -1e30
SCALE = HEAD ** -0.5
SCALE2 = SCALE * math.log2(math.e)
MESH = pl.DeviceIdType.MESH

NT = (((1,), (1,)), ((), ()))
NN = (((1,), (0,)), ((), ()))
TN = (((0,), (0,)), ((), ()))


def dot(a, b, dims):
    return lax.dot_general(a, b, dims, preferred_element_type=jnp.float32)


def kernel(
    order, qf_in, kf_in, vf_in, qb_in, kb_in, vb_in, do_in,
    handed_out, dq_out, dk_out, dv_out,
    kvf, kvb, qf, qb, do, att, dq, part, own, got, total, blank,
    in_sem, kv_sem, out_sem, g_send, g_recv, r_send, r_recv, h_send, h_recv,
):
    pipe, pipes = lax.axis_index("pipe"), lax.axis_size("pipe")
    blk, blks = lax.axis_index("blk"), lax.axis_size("blk")
    uly = lax.axis_index("uly")
    y_hi = lax.rem(blk, 2)
    z, planes = blk // 2, blks // 2
    even = y_hi == 0
    odd = y_hi == 1

    partner = {"uly": 1 - uly}
    cross = {"blk": blk + 1 - 2 * y_hi, "uly": 1 - uly}
    above = {"blk": lax.rem(blk + 2, blks)}
    below = {"blk": lax.rem(blk + blks - 2, blks)}
    after = {"pipe": lax.rem(pipe + 1, pipes)}
    before = {"pipe": lax.rem(pipe + pipes - 1, pipes)}

    barrier = pltpu.get_barrier_semaphore()
    for peer in (partner, cross, above, below, after, before):
        pl.semaphore_signal(barrier, inc=1, device_id=peer, device_id_type=MESH)

    loads = [
        pltpu.make_async_copy(kb_in, kvb.at[0, 0], kv_sem.at[0]),
        pltpu.make_async_copy(vb_in, kvb.at[0, 1], kv_sem.at[1]),
        pltpu.make_async_copy(kf_in, kvf.at[0, 0], kv_sem.at[2]),
        pltpu.make_async_copy(vf_in, kvf.at[0, 1], kv_sem.at[3]),
        pltpu.make_async_copy(qb_in, qb, in_sem.at[0]),
        pltpu.make_async_copy(do_in, do, in_sem.at[1]),
        pltpu.make_async_copy(qf_in, qf, in_sem.at[2]),
    ]
    for load in loads:
        load.start()

    target = {1: partner, 2: above, 3: cross, 4: partner, 5: cross, 6: above, 7: partner}
    back = {1: partner, 2: below, 3: cross, 4: partner, 5: cross, 6: below, 7: partner}

    def message(phase, r, c, source):
        kv = (kvb, kvf)[phase]
        return pltpu.make_async_remote_copy(
            src_ref=kv.at[source, c],
            dst_ref=kv.at[r, c],
            send_sem=g_send.at[phase, c, r],
            recv_sem=g_recv.at[phase, c, r],
            device_id=target[r],
            device_id_type=MESH,
        )

    def forward(phase, arrived, *sends):
        for c in range(2):
            if arrived:
                message(phase, arrived, c, 0).wait_recv()
            for r in sends:
                message(phase, r, c, arrived).start()

    def gather_own(phase):
        forward(phase, 0, 1, 2)

        @pl.when(even)
        def _():
            forward(phase, 0, 3)

    def gather_first(phase):
        @pl.when(even)
        def _():
            forward(phase, 2, 4, 5)
            forward(phase, 1)

        @pl.when(odd)
        def _():
            forward(phase, 2, 3)
            forward(phase, 1, 6)

    def gather_second(phase):
        @pl.when(even)
        def _():
            forward(phase, 3, 6)

        @pl.when(odd)
        def _():
            forward(phase, 3, 4)

    def gather_third(phase):
        @pl.when(even)
        def _():
            forward(phase, 6, 7)
            forward(phase, 4)
            forward(phase, 5)

        @pl.when(odd)
        def _():
            forward(phase, 6, 5)
            forward(phase, 5, 7)
            forward(phase, 4)

    def gather_last(phase):
        forward(phase, 7)

    def term(g, r):
        return pltpu.make_async_remote_copy(
            src_ref=part.at[g, r],
            dst_ref=got.at[g, r],
            send_sem=r_send.at[g, r],
            recv_sem=r_recv.at[g, r],
            device_id=back[r],
            device_id_type=MESH,
        )

    def take(g, r, into):
        term(g, r).wait_recv()
        part[g, into] = (
            part[g, into].astype(jnp.float32) + got[g, r].astype(jnp.float32)
        ).astype(jnp.bfloat16)

    def return_first(g):
        term(g, 7).start()
        term(g, 4).start()

        @pl.when(even)
        def _():
            term(g, 5).start()
            term(g, 1).start()

    def return_second(g):
        @pl.when(even)
        def _():
            take(g, 7, 6)
            term(g, 6).start()
            take(g, 4, 2)

        @pl.when(odd)
        def _():
            take(g, 7, 5)
            term(g, 5).start()
            take(g, 4, 3)
            term(g, 3).start()
            take(g, 5, 6)
            term(g, 6).start()

    def return_third(g):
        @pl.when(even)
        def _():
            take(g, 6, 3)
            term(g, 3).start()
            take(g, 5, 2)
            term(g, 2).start()

        @pl.when(odd)
        def _():
            take(g, 6, 1)
            term(g, 1).start()

    def return_fourth(g):
        @pl.when(odd)
        def _():
            take(g, 3, 2)
            term(g, 2).start()

    y = 2 * y_hi + uly
    col_p, col_x, col_d = 2 * y_hi + 1 - uly, 3 - y, 2 * (1 - y_hi) + uly
    plane = [4 * lax.rem(z + planes - k, planes) for k in range(3)]
    o = 1 - y_hi
    held = [
        plane[0] + y,
        plane[0] + col_p,
        plane[1] + y,
        o * plane[1] + y_hi * plane[0] + col_x,
        o * (plane[1] + col_p) + y_hi * (plane[0] + col_d),
        plane[1] + o * col_d + y_hi * col_x,
        o * (plane[2] + col_x) + y_hi * (plane[1] + col_p),
        o * plane[2] + y_hi * plane[1] + col_d,
    ]
    mine = order[held[0]]
    offsets = [None] + [jnp.where(order[held[r]] < mine, 0.0, NEG) for r in range(1, SLOTS_SEEN)]

    def stacked(ref, g):
        return jnp.concatenate(
            [ref[:, pl.ds(pl.multiple_of(g * WIDE + h * HEAD, HEAD), HEAD)] for h in range(GQA)], axis=0
        )

    def keys(ref, c, g):
        return ref[:, c, :, pl.ds(pl.multiple_of(g * HEAD, HEAD), HEAD)].reshape(KEYS, HEAD)

    def raised(k, q):
        raw = dot(k, q, NT) * SCALE2
        key = lax.broadcasted_iota(jnp.int32, (TOK, ROWS), 0)
        row = lax.broadcasted_iota(jnp.int32, (TOK, ROWS), 1) % TOK
        pieces = [jnp.where(key <= row, raw[:TOK], NEG)]
        for r in range(1, SLOTS_SEEN):
            pieces.append(raw[r * TOK:(r + 1) * TOK] + offsets[r])
        scores = jnp.concatenate(pieces, axis=0)
        p = jnp.exp2(scores - jnp.max(scores, axis=0, keepdims=True))
        return p, 1.0 / jnp.sum(p, axis=0, keepdims=True)

    def spread(ref, g, value):
        for h in range(GQA):
            ref[:, pl.ds(pl.multiple_of(g * WIDE + h * HEAD, HEAD), HEAD)] = value[h * TOK:(h + 1) * TOK]

    def columns(ref, g):
        return ref.at[:, pl.ds(pl.multiple_of(g * WIDE, WIDE), WIDE)]

    def grad_copy(g):
        return pltpu.make_async_copy(columns(dq, g), columns(dq_out, g), out_sem.at[g])

    def blank_copy(g):
        return pltpu.make_async_copy(blank, columns(handed_out, g), out_sem.at[KVH + g])

    def hand(g):
        return pltpu.make_async_remote_copy(
            src_ref=columns(att, g),
            dst_ref=columns(handed_out, g),
            send_sem=h_send.at[g],
            recv_sem=h_recv.at[g],
            device_id=after,
            device_id_type=MESH,
        )

    def backward(g):
        k, v = keys(kvb, 0, g), keys(kvb, 1, g)
        q, up = stacked(qb, g), stacked(do, g)
        p, inverse = raised(k, q)
        p = p * inverse
        dp = dot(v, up, NT)
        delta = jnp.sum(p * dp, axis=0, keepdims=True)
        ds = (p * (dp - delta)).astype(jnp.bfloat16)
        dv = dot(p.astype(jnp.bfloat16), up, NN)
        dk = dot(ds, q, NN) * SCALE
        own[g, 0] = dk[:TOK]
        own[g, 1] = dv[:TOK]
        part[g, :, 0] = dk.reshape(SLOTS_SEEN, TOK, HEAD).astype(jnp.bfloat16)
        part[g, :, 1] = dv.reshape(SLOTS_SEEN, TOK, HEAD).astype(jnp.bfloat16)
        grad = dot(k, ds, TN) * SCALE
        spread(dq, g, grad.T.astype(jnp.bfloat16))
        grad_copy(g).start()

    def forwards(g):
        k, v = keys(kvf, 0, g), keys(kvf, 1, g)
        p, inverse = raised(k, stacked(qf, g))
        weighted = dot(v, p.astype(jnp.bfloat16), TN) * inverse
        spread(att, g, weighted.T.astype(jnp.bfloat16))

        @pl.when(pipe < pipes - 1)
        def _():
            hand(g).start()

    loads[0].wait()
    loads[1].wait()
    pl.semaphore_wait(barrier, 6)
    gather_own(0)

    @pl.when(pipe == 0)
    def _():
        blank[...] = jnp.zeros_like(blank)
        for g in range(KVH):
            blank_copy(g).start()

    gather_first(0)
    gather_second(0)
    gather_third(0)
    loads[2].wait()
    loads[3].wait()
    gather_own(1)
    gather_last(0)
    loads[4].wait()
    loads[5].wait()
    loads[6].wait()

    def step(t, carry):
        @pl.when(t < KVH)
        def _():
            backward(t)
            return_first(t)

        @pl.when(t >= KVH)
        def _():
            forwards(t - KVH)

        @pl.when(t == 0)
        def _():
            gather_first(1)

        @pl.when(t == 1)
        def _():
            gather_second(1)

        @pl.when(t == 2)
        def _():
            gather_third(1)

        @pl.when(t == 3)
        def _():
            gather_last(1)

        @pl.when((t >= 1) & (t < KVH + 1))
        def _():
            return_second(t - 1)

        @pl.when((t >= 2) & (t < KVH + 2))
        def _():
            return_third(t - 2)

        @pl.when((t >= 3) & (t < KVH + 3))
        def _():
            return_fourth(t - 3)

        return carry

    lax.fori_loop(0, 2 * KVH, step, 0)

    for g in range(KVH):
        sums = own[g]
        for r in (1, 2):
            term(g, r).wait_recv()
            sums = sums + got[g, r].astype(jnp.float32)

        @pl.when(odd)
        def _():
            total[:, :, g * HEAD:(g + 1) * HEAD] = sums.astype(jnp.bfloat16)

        @pl.when(even)
        def _():
            term(g, 3).wait_recv()
            full = sums + got[g, 3].astype(jnp.float32)
            total[:, :, g * HEAD:(g + 1) * HEAD] = full.astype(jnp.bfloat16)

    stores = [
        pltpu.make_async_copy(total.at[0], dk_out, kv_sem.at[0]),
        pltpu.make_async_copy(total.at[1], dv_out, kv_sem.at[1]),
    ]
    for store in stores:
        store.start()
    for g in range(KVH):
        grad_copy(g).wait()
        for r in range(1, SLOTS_SEEN):
            term(g, r).wait_send()
    for phase in range(2):
        for c in range(2):
            for r in range(1, SLOTS_SEEN):
                message(phase, r, c, 0).wait_send()

    @pl.when(pipe < pipes - 1)
    def _():
        for g in range(KVH):
            hand(g).wait_send()

    @pl.when(pipe > 0)
    def _():
        for g in range(KVH):
            hand(g).wait_recv()

    @pl.when(pipe == 0)
    def _():
        for g in range(KVH):
            blank_copy(g).wait()

    for store in stores:
        store.wait()


def local(order, *arrays):
    bf16 = jnp.bfloat16
    wide, narrow = (TOK, KVH * WIDE), (TOK, KVH * HEAD)
    anywhere = pl.BlockSpec(memory_space=pl.ANY)
    dma = pltpu.SemaphoreType.DMA
    outs = pl.pallas_call(
        kernel,
        out_shape=[jax.ShapeDtypeStruct(s, bf16) for s in (wide, wide, narrow, narrow)],
        in_specs=[pl.BlockSpec(memory_space=pltpu.SMEM)] + [anywhere] * 7,
        out_specs=[anywhere] * 4,
        scratch_shapes=[
            pltpu.VMEM((SLOTS_SEEN, 2) + narrow, bf16),
            pltpu.VMEM((SLOTS_SEEN, 2) + narrow, bf16),
            pltpu.VMEM(wide, bf16),
            pltpu.VMEM(wide, bf16),
            pltpu.VMEM(wide, bf16),
            pltpu.VMEM(wide, bf16),
            pltpu.VMEM(wide, bf16),
            pltpu.VMEM((KVH, SLOTS_SEEN, 2, TOK, HEAD), bf16),
            pltpu.VMEM((KVH, 2, TOK, HEAD), jnp.float32),
            pltpu.VMEM((KVH, SLOTS_SEEN, 2, TOK, HEAD), bf16),
            pltpu.VMEM((2,) + narrow, bf16),
            pltpu.VMEM((TOK, WIDE), bf16),
            dma((3,)),
            dma((4,)),
            dma((2 * KVH,)),
            dma((2, 2, SLOTS_SEEN)),
            dma((2, 2, SLOTS_SEEN)),
            dma((KVH, SLOTS_SEEN)),
            dma((KVH, SLOTS_SEEN)),
            dma((KVH,)),
            dma((KVH,)),
        ],
        compiler_params=pltpu.CompilerParams(
            collective_id=0, has_side_effects=True, vmem_limit_bytes=40 * 1024 * 1024
        ),
    )(order, *[a[0] for a in arrays])
    return tuple(out[None] for out in outs)


def solution(mesh):
    split = P("pipe", ("blk", "uly"), None)
    return jax.shard_map(
        local,
        mesh=mesh,
        in_specs=(P(),) + (split,) * 7,
        out_specs=(split,) * 4,
        check_vma=False,
    )
```

```python
import functools
import math

import jax
import jax.numpy as jnp
from jax import lax
from jax.experimental import pallas as pl
from jax.experimental.pallas import tpu as pltpu
from jax.sharding import PartitionSpec as P

HEAD = 128
GQA = 8
KVH = 4
TOK = 64
SLOTS_SEEN = 8
KEYS = SLOTS_SEEN * TOK
ROWS = GQA * TOK
WIDE = GQA * HEAD
NEG = -1e30
SCALE = HEAD ** -0.5
SCALE2 = SCALE * math.log2(math.e)
VMEM_BYTES = 60 * 1024 * 1024
UNITS = ((0, 0, 1), (0, 1, 1), (0, 2, 1), (0, 3, 1), (1, 0, 2), (1, 2, 2))
PAIRED = ((0, 0, 1), (0, 2, 1), )
RETURNS = ("r1", "t7", "t6", "t45", "t5", "t3", "t4")
EVEN = (
    (("own", 3), ("own", 2), ("own", 0), ("own", 1), ("own", 5), ("f2", 2), ("f2", 0), ("f3", 0), ("own", 4),
     ("f3", 2), ("f2", 1), ("f7", 0), ("f3", 1), ("f2", 3), ("f7", 1), ("f7", 2), ("f2", 5), ("f3", 3), ("f2", 4),
     ("last", 0),),
    (("f7", 3), ("r1", 0), ("last", 1),),
    (("r1", 1), ("last", 2), ("f3", 4),),
    (("t7", 0), ("t6", 0), ("f7", 4), ("r1", 2), ("last", 3),),
    (("r1", 3), ("t7", 1), ("f3", 5), ("t7", 2), ("t6", 1), ("t45", 1), ("f7", 5), ("last", 4),),
    (("t7", 3), ("t6", 2),),
    (("last", 5), ("t45", 0), ("t6", 3),),
    (("t45", 3), ("t45", 2),),
    (),
)
ODD = (
    (("own", 0), ("own", 1), ("own", 2), ("own", 3), ("own", 4), ("f2", 0), ("f1", 1), ("f2", 1), ("f1", 0),
     ("f3", 0), ("f2", 2), ("f1", 3), ("own", 5), ("f1", 2), ("f2", 3), ("f3", 1), ("f6", 1), ("f7", 0), ("f6", 0),
     ("f1", 4), ("f3", 3), ("f6", 3), ("f7", 1), ("f1", 5), ("f3", 2), ("f2", 4), ("last", 0), ("f3", 4), ("f7", 2),
     ("f6", 2),),
    (("f6", 4), ("f7", 3), ("f2", 5), ("last", 1),),
    (("f3", 5), ("r1", 1), ("f6", 5), ("f7", 4), ("last", 2), ("r1", 0),),
    (("r1", 2), ("last", 3),),
    (("t7", 0), ("r1", 3), ("t7", 2), ("t3", 0), ("last", 4), ("t5", 0), ("f7", 5),),
    (("t4", 0), ("t5", 1), ("t7", 1), ("t7", 3), ("t5", 2),),
    (("t4", 2), ("t6", 0), ("last", 5), ("t5", 3), ("t3", 1),),
    (("t3", 2), ("t6", 2), ("t4", 1), ("t6", 1),),
    (("t4", 3), ("t3", 3), ("t6", 3),),
)
MESH = pl.DeviceIdType.MESH

NT = (((1,), (1,)), ((), ()))
NN = (((1,), (0,)), ((), ()))
TN = (((0,), (0,)), ((), ()))


def dot(a, b, dims):
    return lax.dot_general(a, b, dims, preferred_element_type=jnp.float32)


def kernel(
    order, qf_in, kf_in, vf_in, qb_in, kb_in, vb_in, do_in,
    handed_out, dq_out, dk_out, dv_out,
    kvf, kvb, qf, qb, do, att, dq, part, own, got, total, blank,
    in_sem, kv_sem, out_sem, g_send, g_recv, r_send, r_recv, h_send, h_recv,
):
    pipe, pipes = lax.axis_index("pipe"), lax.axis_size("pipe")
    blk, blks = lax.axis_index("blk"), lax.axis_size("blk")
    uly = lax.axis_index("uly")
    y_hi = lax.rem(blk, 2)
    z, planes = blk // 2, blks // 2
    even = y_hi == 0
    odd = y_hi == 1

    partner = {"uly": 1 - uly}
    cross = {"blk": blk + 1 - 2 * y_hi, "uly": 1 - uly}
    above = {"blk": lax.rem(blk + 2, blks)}
    below = {"blk": lax.rem(blk + blks - 2, blks)}
    after = {"pipe": lax.rem(pipe + 1, pipes)}
    before = {"pipe": lax.rem(pipe + pipes - 1, pipes)}

    barrier = pltpu.get_barrier_semaphore()
    for peer in (partner, cross, above, below, after, before):
        pl.semaphore_signal(barrier, inc=1, device_id=peer, device_id_type=MESH)

    kv_loads = {}
    for phase, sources in enumerate(((kb_in, vb_in), (kf_in, vf_in))):
        for g in range(KVH):
            kv_loads[phase, g] = [
                pltpu.make_async_copy(
                    source.at[:, g * HEAD:(g + 1) * HEAD], (kvb, kvf)[phase].at[0, g, c], kv_sem.at[phase, g, c]
                )
                for c, source in enumerate(sources)
            ]
    loads = [
        pltpu.make_async_copy(qb_in, qb, in_sem.at[0]),
        pltpu.make_async_copy(do_in, do, in_sem.at[1]),
        pltpu.make_async_copy(qf_in, qf, in_sem.at[2]),
    ]
    for pair in kv_loads.values():
        for load in pair:
            load.start()
    for load in loads:
        load.start()

    target = {1: partner, 2: above, 3: cross, 4: partner, 5: cross, 6: above, 7: above}
    back = {1: partner, 2: below, 3: cross, 4: partner, 5: cross, 6: below, 7: below}

    def paired(unit):
        return unit in PAIRED

    def message(unit, r, source):
        phase, head, count = unit
        kv = (kvb, kvf)[phase]
        return pltpu.make_async_remote_copy(
            src_ref=kv.at[source, pl.ds(head, count)],
            dst_ref=kv.at[r, pl.ds(head, count)],
            send_sem=g_send.at[phase, head, r],
            recv_sem=g_recv.at[phase, head, r],
            device_id=partner if r == 7 and paired(unit) else target[r],
            device_id_type=MESH,
        )

    def forward(unit, arrived, *sends):
        if arrived:
            message(unit, arrived, 0).wait_recv()
        for r in sends:
            message(unit, r, arrived).start()

    def own_slot(unit, *sends):
        phase, head, count = unit
        for g in range(head, head + count):
            for load in kv_loads[phase, g]:
                load.wait()
        forward(unit, 0, *sends)

    def last_slots(unit, *slots):
        for r in slots:
            forward(unit, r)

    def term(g, r):
        return pltpu.make_async_remote_copy(
            src_ref=part.at[g, r],
            dst_ref=got.at[g, r],
            send_sem=r_send.at[g, r],
            recv_sem=r_recv.at[g, r],
            device_id=back[r],
            device_id_type=MESH,
        )

    def take(g, r, into):
        term(g, r).wait_recv()
        part[g, into] = (
            part[g, into].astype(jnp.float32) + got[g, r].astype(jnp.float32)
        ).astype(jnp.bfloat16)

    def gather_moves(unit):
        pair = paired(unit)
        return {
            "own": (lambda: own_slot(unit, 3, 2, 1), lambda: own_slot(unit, 2, 1)),
            "f1": (None, lambda: forward(unit, 1, 6)),
            "f2": (lambda: forward(unit, 2, 5, 4), lambda: forward(unit, 2, 3)),
            "f3": (lambda: forward(unit, 3, 6), lambda: forward(unit, 3, 4)),
            "f6": (None, lambda: forward(unit, 6, 5)),
            "f7": (lambda: forward(unit, 6 if pair else 5, 7), lambda: forward(unit, 5 if pair else 4, 7)),
            "last": (
                lambda: last_slots(unit, 1, 4, 5 if pair else 6, 7),
                lambda: last_slots(unit, 4 if pair else 5, 7),
            ),
        }

    def back_send(g, *slots):
        for r in slots:
            term(g, r).start()

    def back_sum(g, into, *slots):
        for r in slots:
            take(g, r, into)
        term(g, into).start()

    def return_moves(g):
        return {
            "r1": (lambda: back_send(g, 7, 4, 6, 1), lambda: back_send(g, 5, 7)),
            "t7": (lambda: back_sum(g, 5, 7), lambda: back_sum(g, 4, 7)),
            "t6": (lambda: back_sum(g, 3, 6), lambda: back_sum(g, 1, 6)),
            "t45": (lambda: back_sum(g, 2, 4, 5), None),
            "t5": (None, lambda: back_sum(g, 6, 5)),
            "t3": (None, lambda: back_sum(g, 2, 3)),
            "t4": (None, lambda: back_sum(g, 3, 4)),
        }

    def run(k):
        for parity, table in enumerate((EVEN, ODD)):
            @pl.when(y_hi == parity)
            def _():
                for name, index in table[k]:
                    moves = return_moves(index) if name in RETURNS else gather_moves(UNITS[index])
                    moves[name][parity]()

    y = 2 * y_hi + uly
    col_p, col_x, col_d = 2 * y_hi + 1 - uly, 3 - y, 2 * (1 - y_hi) + uly
    plane = [4 * lax.rem(z + planes - k, planes) for k in range(3)]
    o = 1 - y_hi
    held = [
        plane[0] + y,
        plane[0] + col_p,
        plane[1] + y,
        o * plane[1] + y_hi * plane[0] + col_x,
        o * (plane[1] + col_p) + y_hi * (plane[0] + col_d),
        plane[1] + o * col_d + y_hi * col_x,
        o * (plane[2] + col_x) + y_hi * (plane[1] + col_p),
        o * plane[2] + y_hi * plane[1] + col_d,
    ]
    mine = order[held[0]]
    offsets = [None] + [jnp.where(order[held[r]] < mine, 0.0, NEG) for r in range(1, SLOTS_SEEN)]

    def stacked(ref, g):
        return jnp.concatenate(
            [ref[:, pl.ds(pl.multiple_of(g * WIDE + h * HEAD, HEAD), HEAD)] for h in range(GQA)], axis=0
        )

    def keys(ref, c, g):
        return ref[:, g, c].reshape(KEYS, HEAD)

    def raised(k, q):
        raw = dot(k, q, NT) * SCALE2
        key = lax.broadcasted_iota(jnp.int32, (TOK, ROWS), 0)
        row = lax.broadcasted_iota(jnp.int32, (TOK, ROWS), 1) % TOK
        pieces = [jnp.where(key <= row, raw[:TOK], NEG)]
        for r in range(1, SLOTS_SEEN):
            pieces.append(raw[r * TOK:(r + 1) * TOK] + offsets[r])
        scores = jnp.concatenate(pieces, axis=0)
        p = jnp.exp2(scores - jnp.max(scores, axis=0, keepdims=True))
        return p, 1.0 / jnp.sum(p, axis=0, keepdims=True)

    def spread(ref, g, value):
        for h in range(GQA):
            ref[:, pl.ds(pl.multiple_of(g * WIDE + h * HEAD, HEAD), HEAD)] = value[h * TOK:(h + 1) * TOK]

    def columns(ref, g):
        return ref.at[:, pl.ds(pl.multiple_of(g * WIDE, WIDE), WIDE)]

    def grad_copy(g):
        return pltpu.make_async_copy(columns(dq, g), columns(dq_out, g), out_sem.at[g])

    def blank_copy(g):
        return pltpu.make_async_copy(blank, columns(handed_out, g), out_sem.at[KVH + g])

    def hand(g):
        return pltpu.make_async_remote_copy(
            src_ref=columns(att, g),
            dst_ref=columns(handed_out, g),
            send_sem=h_send.at[g],
            recv_sem=h_recv.at[g],
            device_id=after,
            device_id_type=MESH,
        )

    def backward(g):
        k, v = keys(kvb, 0, g), keys(kvb, 1, g)
        q, up = stacked(qb, g), stacked(do, g)
        p, inverse = raised(k, q)
        p = p * inverse
        dp = dot(v, up, NT)
        delta = jnp.sum(p * dp, axis=0, keepdims=True)
        ds = (p * (dp - delta)).astype(jnp.bfloat16)
        dv = dot(p.astype(jnp.bfloat16), up, NN)
        dk = dot(ds, q, NN) * SCALE
        own[g, 0] = dk[:TOK]
        own[g, 1] = dv[:TOK]
        part[g, :, 0] = dk.reshape(SLOTS_SEEN, TOK, HEAD).astype(jnp.bfloat16)
        part[g, :, 1] = dv.reshape(SLOTS_SEEN, TOK, HEAD).astype(jnp.bfloat16)
        grad = dot(k, ds, TN) * SCALE
        spread(dq, g, grad.T.astype(jnp.bfloat16))
        grad_copy(g).start()

    def forwards(g):
        k, v = keys(kvf, 0, g), keys(kvf, 1, g)
        p, inverse = raised(k, stacked(qf, g))
        weighted = dot(v, p.astype(jnp.bfloat16), TN) * inverse
        spread(att, g, weighted.T.astype(jnp.bfloat16))

        @pl.when(pipe < pipes - 1)
        def _():
            hand(g).start()

    pl.semaphore_wait(barrier, 6)
    run(0)
    for load in loads:
        load.wait()

    @pl.when(pipe == 0)
    def _():
        blank[...] = jnp.zeros_like(blank)
        for g in range(KVH):
            blank_copy(g).start()

    def step(t, carry):
        @pl.when(t < KVH)
        def _():
            backward(t)

        @pl.when(t >= KVH)
        def _():
            forwards(t - KVH)

        for k in range(2 * KVH):
            @pl.when(t == k)
            def _():
                run(k + 1)

        return carry

    lax.fori_loop(0, 2 * KVH, step, 0)

    for g in range(KVH):
        sums = own[g]
        for r in (1, 2):
            term(g, r).wait_recv()
            sums = sums + got[g, r].astype(jnp.float32)

        @pl.when(odd)
        def _():
            total[:, :, g * HEAD:(g + 1) * HEAD] = sums.astype(jnp.bfloat16)

        @pl.when(even)
        def _():
            term(g, 3).wait_recv()
            full = sums + got[g, 3].astype(jnp.float32)
            total[:, :, g * HEAD:(g + 1) * HEAD] = full.astype(jnp.bfloat16)

    stores = [
        pltpu.make_async_copy(total.at[0], dk_out, out_sem.at[2 * KVH]),
        pltpu.make_async_copy(total.at[1], dv_out, out_sem.at[2 * KVH + 1]),
    ]
    for store in stores:
        store.start()
    for g in range(KVH):
        grad_copy(g).wait()
        for r in range(1, SLOTS_SEEN):
            term(g, r).wait_send()
    for unit in UNITS:
        for r in range(1, SLOTS_SEEN):
            message(unit, r, 0).wait_send()

    @pl.when(pipe < pipes - 1)
    def _():
        for g in range(KVH):
            hand(g).wait_send()

    @pl.when(pipe > 0)
    def _():
        for g in range(KVH):
            hand(g).wait_recv()

    @pl.when(pipe == 0)
    def _():
        for g in range(KVH):
            blank_copy(g).wait()

    for store in stores:
        store.wait()


def settle(*refs):
    ins, outs, held, sems = refs[:4], refs[4:8], refs[8:12], refs[12]
    fetched = [pltpu.make_async_copy(ins[i], held[i], sems.at[0, i]) for i in range(4)]
    stored = [pltpu.make_async_copy(held[i], outs[i], sems.at[1, i]) for i in range(4)]
    for copy in fetched:
        copy.start()
    for fetch, store in zip(fetched, stored):
        fetch.wait()
        store.start()
    for copy in stored:
        copy.wait()


def local(order, *arrays):
    bf16 = jnp.bfloat16
    wide, narrow = (TOK, KVH * WIDE), (TOK, KVH * HEAD)
    anywhere = pl.BlockSpec(memory_space=pl.ANY)
    in_hbm = pl.BlockSpec(memory_space=pltpu.HBM)
    dma = pltpu.SemaphoreType.DMA
    outs = pl.pallas_call(
        kernel,
        out_shape=[jax.ShapeDtypeStruct(s, bf16) for s in (wide, wide, narrow, narrow)],
        in_specs=[pl.BlockSpec(memory_space=pltpu.SMEM)] + [in_hbm] * 7,
        out_specs=[anywhere] * 4,
        scratch_shapes=[
            pltpu.VMEM((SLOTS_SEEN, KVH, 2, TOK, HEAD), bf16),
            pltpu.VMEM((SLOTS_SEEN, KVH, 2, TOK, HEAD), bf16),
            pltpu.VMEM(wide, bf16),
            pltpu.VMEM(wide, bf16),
            pltpu.VMEM(wide, bf16),
            pltpu.VMEM(wide, bf16),
            pltpu.VMEM(wide, bf16),
            pltpu.VMEM((KVH, SLOTS_SEEN, 2, TOK, HEAD), bf16),
            pltpu.VMEM((KVH, 2, TOK, HEAD), jnp.float32),
            pltpu.VMEM((KVH, SLOTS_SEEN, 2, TOK, HEAD), bf16),
            pltpu.VMEM((2,) + narrow, bf16),
            pltpu.VMEM((TOK, WIDE), bf16),
            dma((3,)),
            dma((2, KVH, 2)),
            dma((2 * KVH + 2,)),
            dma((2, KVH, SLOTS_SEEN)),
            dma((2, KVH, SLOTS_SEEN)),
            dma((KVH, SLOTS_SEEN)),
            dma((KVH, SLOTS_SEEN)),
            dma((KVH,)),
            dma((KVH,)),
        ],
        compiler_params=pltpu.CompilerParams(
            collective_id=0, has_side_effects=True, vmem_limit_bytes=VMEM_BYTES
        ),
    )(order, *[a[0] for a in arrays])
    outs = pl.pallas_call(
        settle,
        out_shape=[jax.ShapeDtypeStruct(out.shape, out.dtype) for out in outs],
        in_specs=[in_hbm] * 4,
        out_specs=[in_hbm] * 4,
        scratch_shapes=[pltpu.VMEM(out.shape, out.dtype) for out in outs] + [dma((2, 4))],
        compiler_params=pltpu.CompilerParams(vmem_limit_bytes=VMEM_BYTES),
    )(*outs)
    return tuple(out[None] for out in outs)


def solution(mesh):
    split = P("pipe", ("blk", "uly"), None)
    return jax.shard_map(
        local,
        mesh=mesh,
        in_specs=(P(),) + (split,) * 7,
        out_specs=(split,) * 4,
        check_vma=False,
    )
```

```python
import functools
import math

import jax
import jax.numpy as jnp
from jax import lax
from jax.experimental import pallas as pl
from jax.experimental.pallas import tpu as pltpu
from jax.sharding import PartitionSpec as P

HEAD = 128
GQA = 8
KVH = 4
TOK = 64
SLOTS_SEEN = 8
KEYS = SLOTS_SEEN * TOK
ROWS = GQA * TOK
WIDE = GQA * HEAD
NEG = -1e30
SCALE = HEAD ** -0.5
SCALE2 = SCALE * math.log2(math.e)
VMEM_BYTES = 60 * 1024 * 1024
TREES = (
    (
        {1: (0, 0, "P"), 2: (0, 0, "U"), 3: (1, 2, "X"), 4: (0, 2, "P"), 5: (1, 2, "D"), 6: (0, 3, "U"), 7: (0, 5, "U")},
        {1: (1, 0, "P"), 2: (1, 0, "U"), 3: (0, 0, "X"), 4: (1, 3, "P"), 5: (0, 2, "X"), 6: (1, 1, "U"), 7: (0, 1, "ZX")},
    ),
    (
        {1: (0, 0, "P"), 2: (0, 0, "U"), 3: (1, 2, "X"), 4: (0, 2, "P"), 5: (1, 1, "ZX"), 6: (0, 3, "U"), 7: (0, 5, "U")},
        {1: (1, 0, "P"), 2: (1, 0, "U"), 3: (0, 0, "X"), 4: (1, 3, "P"), 5: (1, 3, "U"), 6: (1, 1, "U"), 7: (1, 4, "U")},
    ),
    (
        {1: (0, 0, "P"), 2: (0, 0, "U"), 3: (1, 0, "ZX"), 4: (0, 2, "P"), 5: (1, 2, "D"), 6: (1, 2, "ZX"), 7: (0, 3, "ZP")},
        {1: (1, 0, "P"), 2: (1, 0, "U"), 3: (0, 0, "X"), 4: (1, 3, "P"), 5: (0, 2, "X"), 6: (1, 1, "U"), 7: (0, 1, "ZX")},
    ),
)
UNITS = ((0, 0, 1, 0), (0, 1, 1, 0), (0, 2, 1, 0), (0, 3, 1, 0), (1, 0, 2, 1), (1, 2, 2, 1))
BACK = (2, 2, 2, 2)
WAYS = tuple(sorted({way for tree in TREES for slots in tree for _, _, way in slots.values()}))


def fed(tree, parity, slot):
    found = [
        (p, r, way) for p in range(2) for r, (q, source, way) in tree[p].items() if (q, source) == (parity, slot)
    ]
    return sorted(found, key=lambda f: -chain(tree, f[0], f[1]))


def chain(tree, parity, slot):
    return 1 + max([chain(tree, p, r) for p, r, _ in fed(tree, parity, slot)], default=0)


EVEN = (
    (("fwd", 0, 3), ("fwd", 0, 0), ("fwd", 0, 1), ("fwd", 0, 4), ("fwd", 0, 2), ("fwd", 2, 0), ("fwd", 1, 0),
     ("fwd", 0, 5), ("fwd", 1, 1), ("fwd", 2, 4), ("fwd", 3, 0), ("fwd", 2, 2), ("fwd", 5, 0), ("fwd", 2, 1),
     ("fwd", 1, 2), ("fwd", 2, 3), ("fwd", 3, 1), ("fwd", 1, 3), ("fwd", 5, 1), ("fwd", 3, 2), ("fwd", 2, 5),
     ("last", 0, 0),),
    (("fwd", 5, 2), ("fwd", 5, 4), ("ret", 4, 0), ("ret", 7, 0), ("ret", 5, 0), ("ret", 6, 0), ("last", 0, 1),
     ("fwd", 3, 3), ("fwd", 5, 3),),
    (("fwd", 3, 4), ("ret", 7, 1), ("ret", 6, 1), ("ret", 5, 1), ("ret", 4, 1), ("last", 0, 2),),
    (("fwd", 5, 5), ("ret", 3, 0), ("ret", 7, 2), ("fwd", 3, 5), ("ret", 5, 2), ("ret", 6, 2), ("last", 0, 3),),
    (("ret", 7, 3), ("ret", 5, 3), ("ret", 4, 3), ("ret", 6, 3), ("ret", 3, 1), ("last", 0, 4), ("ret", 4, 2),),
    (),
    (("ret", 2, 0), ("ret", 2, 1), ("ret", 1, 0), ("ret", 1, 1), ("last", 0, 5), ("ret", 3, 2),),
    (("ret", 1, 3), ("ret", 1, 2), ("ret", 3, 3),),
    (("ret", 2, 2), ("ret", 2, 3),),
)
ODD = (
    (("fwd", 0, 0), ("fwd", 0, 1), ("fwd", 0, 2), ("fwd", 0, 4), ("fwd", 2, 0), ("fwd", 1, 0), ("fwd", 0, 3),
     ("fwd", 2, 1), ("fwd", 2, 2), ("fwd", 1, 1), ("fwd", 1, 2), ("fwd", 3, 0), ("fwd", 0, 5), ("fwd", 1, 4),
     ("fwd", 1, 3), ("fwd", 3, 1), ("fwd", 2, 3), ("fwd", 3, 2), ("fwd", 2, 4), ("last", 0, 0), ("fwd", 1, 5),
     ("fwd", 3, 4),),
    (("fwd", 2, 5), ("fwd", 3, 3), ("fwd", 3, 5), ("last", 0, 1),),
    (("ret", 5, 1), ("last", 0, 2), ("ret", 7, 0),),
    (("ret", 6, 1), ("ret", 7, 1), ("fwd", 4, 4), ("last", 0, 3), ("ret", 5, 0), ("ret", 4, 0), ("ret", 6, 0),),
    (("ret", 7, 3), ("ret", 6, 2), ("ret", 4, 3), ("ret", 4, 2), ("fwd", 4, 5), ("ret", 5, 2), ("ret", 5, 3),
     ("ret", 7, 2), ("ret", 4, 1), ("ret", 3, 0), ("last", 0, 4),),
    (("ret", 2, 0), ("ret", 3, 3),),
    (("ret", 6, 3), ("ret", 1, 2), ("last", 0, 5),),
    (("ret", 3, 1), ("ret", 1, 1), ("ret", 2, 1), ("ret", 3, 2),),
    (("ret", 1, 0), ("ret", 2, 3), ("ret", 1, 3), ("ret", 2, 2),),
)
MESH = pl.DeviceIdType.MESH

NT = (((1,), (1,)), ((), ()))
NN = (((1,), (0,)), ((), ()))
TN = (((0,), (0,)), ((), ()))


def dot(a, b, dims):
    return lax.dot_general(a, b, dims, preferred_element_type=jnp.float32)


def kernel(
    order, qf_in, kf_in, vf_in, qb_in, kb_in, vb_in, do_in,
    handed_out, dq_out, dk_out, dv_out,
    kvf, kvb, qf, qb, do, att, dq, part, own, got, total, blank,
    in_sem, kv_sem, out_sem, g_send, g_recv, r_send, r_recv, h_send, h_recv,
):
    pipe, pipes = lax.axis_index("pipe"), lax.axis_size("pipe")
    blk, blks = lax.axis_index("blk"), lax.axis_size("blk")
    uly = lax.axis_index("uly")
    y_hi = lax.rem(blk, 2)
    z, planes = blk // 2, blks // 2

    partner = {"uly": 1 - uly}
    flip = blk + 1 - 2 * y_hi

    def ring(group):
        return lax.rem(group + 2 * blks, blks)

    up = {
        "P": partner,
        "X": {"blk": flip, "uly": 1 - uly},
        "D": {"blk": flip},
        "U": {"blk": ring(blk + 2)},
        "ZP": {"blk": ring(blk + 2), "uly": 1 - uly},
        "ZX": {"blk": ring(flip + 2), "uly": 1 - uly},
        "ZZX": {"blk": ring(flip + 4), "uly": 1 - uly},
    }
    down = dict(
        up,
        U={"blk": ring(blk - 2)},
        ZP={"blk": ring(blk - 2), "uly": 1 - uly},
        ZX={"blk": ring(flip - 2), "uly": 1 - uly},
        ZZX={"blk": ring(flip - 4), "uly": 1 - uly},
    )
    after = {"pipe": lax.rem(pipe + 1, pipes)}
    before = {"pipe": lax.rem(pipe + pipes - 1, pipes)}

    barrier = pltpu.get_barrier_semaphore()
    peers = [up[way] for way in WAYS] + [down[way] for way in WAYS if way not in "PXD"] + [after, before]
    for peer in peers:
        pl.semaphore_signal(barrier, inc=1, device_id=peer, device_id_type=MESH)

    kv_loads = {}
    for phase, sources in enumerate(((kb_in, vb_in), (kf_in, vf_in))):
        for g in range(KVH):
            kv_loads[phase, g] = [
                pltpu.make_async_copy(
                    source.at[:, g * HEAD:(g + 1) * HEAD], (kvb, kvf)[phase].at[0, g, c], kv_sem.at[phase, g, c]
                )
                for c, source in enumerate(sources)
            ]
    loads = [
        pltpu.make_async_copy(qb_in, qb, in_sem.at[0]),
        pltpu.make_async_copy(do_in, do, in_sem.at[1]),
        pltpu.make_async_copy(qf_in, qf, in_sem.at[2]),
    ]
    for pair in kv_loads.values():
        for load in pair:
            load.start()
    for load in loads:
        load.start()

    def message(unit, parity, r, way, source=0):
        phase, head, count, _ = unit
        kv = (kvb, kvf)[phase]
        return pltpu.make_async_remote_copy(
            src_ref=kv.at[source, pl.ds(head, count)],
            dst_ref=kv.at[r, pl.ds(head, count)],
            send_sem=g_send.at[phase, head, parity, r],
            recv_sem=g_recv.at[phase, head, r],
            device_id=up[way],
            device_id_type=MESH,
        )

    def arrived(unit, r):
        message(unit, 0, r, "P").wait_recv()

    def send_on(unit, parity, slot):
        phase, head, count, tree = unit
        if slot:
            arrived(unit, slot)
        else:
            for g in range(head, head + count):
                for load in kv_loads[phase, g]:
                    load.wait()
        for p, r, way in fed(TREES[tree], parity, slot):
            message(unit, p, r, way, slot).start()

    def wait_others(unit, parity, _):
        for r in range(1, SLOTS_SEEN):
            if not fed(TREES[unit[3]], parity, r):
                arrived(unit, r)

    def term(g, parity, r):
        return pltpu.make_async_remote_copy(
            src_ref=part.at[g, r],
            dst_ref=got.at[g, parity, r],
            send_sem=r_send.at[g, r],
            recv_sem=r_recv.at[g, parity, r],
            device_id=down[TREES[BACK[g]][parity][r][2]],
            device_id_type=MESH,
        )

    def received(g, parity, slot, sums):
        for p, r, _ in reversed(fed(TREES[BACK[g]], parity, slot)):
            term(g, p, r).wait_recv()
            sums = sums + got[g, p, r].astype(jnp.float32)
        return sums

    def send_back(g, parity, slot):
        if fed(TREES[BACK[g]], parity, slot):
            sums = received(g, parity, slot, part[g, slot].astype(jnp.float32))
            part[g, slot] = sums.astype(jnp.bfloat16)
        term(g, parity, slot).start()

    def run(k):
        for parity, table in enumerate((EVEN, ODD)):
            @pl.when(y_hi == parity)
            def _():
                for name, slot, index in table[k]:
                    if name == "ret":
                        send_back(index, parity, slot)
                    else:
                        {"fwd": send_on, "last": wait_others}[name](UNITS[index], parity, slot)

    y = 2 * y_hi + uly
    col_p, col_x, col_d = 2 * y_hi + 1 - uly, 3 - y, 2 * (1 - y_hi) + uly
    plane = [4 * lax.rem(z + planes - k, planes) for k in range(3)]
    o = 1 - y_hi
    held = [
        plane[0] + y,
        plane[0] + col_p,
        plane[1] + y,
        o * plane[1] + y_hi * plane[0] + col_x,
        o * (plane[1] + col_p) + y_hi * (plane[0] + col_d),
        plane[1] + o * col_d + y_hi * col_x,
        o * (plane[2] + col_x) + y_hi * (plane[1] + col_p),
        o * plane[2] + y_hi * plane[1] + col_d,
    ]
    mine = order[held[0]]
    offsets = [None] + [jnp.where(order[held[r]] < mine, 0.0, NEG) for r in range(1, SLOTS_SEEN)]

    def stacked(ref, g):
        return jnp.concatenate(
            [ref[:, pl.ds(pl.multiple_of(g * WIDE + h * HEAD, HEAD), HEAD)] for h in range(GQA)], axis=0
        )

    def keys(ref, c, g):
        return ref[:, g, c].reshape(KEYS, HEAD)

    def raised(k, q):
        raw = dot(k, q, NT) * SCALE2
        key = lax.broadcasted_iota(jnp.int32, (TOK, ROWS), 0)
        row = lax.broadcasted_iota(jnp.int32, (TOK, ROWS), 1) % TOK
        pieces = [jnp.where(key <= row, raw[:TOK], NEG)]
        for r in range(1, SLOTS_SEEN):
            pieces.append(raw[r * TOK:(r + 1) * TOK] + offsets[r])
        scores = jnp.concatenate(pieces, axis=0)
        p = jnp.exp2(scores - jnp.max(scores, axis=0, keepdims=True))
        return p, 1.0 / jnp.sum(p, axis=0, keepdims=True)

    def spread(ref, g, value):
        for h in range(GQA):
            ref[:, pl.ds(pl.multiple_of(g * WIDE + h * HEAD, HEAD), HEAD)] = value[h * TOK:(h + 1) * TOK]

    def columns(ref, g):
        return ref.at[:, pl.ds(pl.multiple_of(g * WIDE, WIDE), WIDE)]

    def grad_copy(g):
        return pltpu.make_async_copy(columns(dq, g), columns(dq_out, g), out_sem.at[g])

    def blank_copy(g):
        return pltpu.make_async_copy(blank, columns(handed_out, g), out_sem.at[KVH + g])

    def hand(g):
        return pltpu.make_async_remote_copy(
            src_ref=columns(att, g),
            dst_ref=columns(handed_out, g),
            send_sem=h_send.at[g],
            recv_sem=h_recv.at[g],
            device_id=after,
            device_id_type=MESH,
        )

    def backward(g):
        k, v = keys(kvb, 0, g), keys(kvb, 1, g)
        q, up = stacked(qb, g), stacked(do, g)
        p, inverse = raised(k, q)
        p = p * inverse
        dp = dot(v, up, NT)
        delta = jnp.sum(p * dp, axis=0, keepdims=True)
        ds = (p * (dp - delta)).astype(jnp.bfloat16)
        dv = dot(p.astype(jnp.bfloat16), up, NN)
        dk = dot(ds, q, NN) * SCALE
        own[g, 0] = dk[:TOK]
        own[g, 1] = dv[:TOK]
        part[g, :, 0] = dk.reshape(SLOTS_SEEN, TOK, HEAD).astype(jnp.bfloat16)
        part[g, :, 1] = dv.reshape(SLOTS_SEEN, TOK, HEAD).astype(jnp.bfloat16)
        grad = dot(k, ds, TN) * SCALE
        spread(dq, g, grad.T.astype(jnp.bfloat16))
        grad_copy(g).start()

    def forwards(g):
        k, v = keys(kvf, 0, g), keys(kvf, 1, g)
        p, inverse = raised(k, stacked(qf, g))
        weighted = dot(v, p.astype(jnp.bfloat16), TN) * inverse
        spread(att, g, weighted.T.astype(jnp.bfloat16))

        @pl.when(pipe < pipes - 1)
        def _():
            hand(g).start()

    pl.semaphore_wait(barrier, len(peers))
    run(0)
    for load in loads:
        load.wait()

    @pl.when(pipe == 0)
    def _():
        blank[...] = jnp.zeros_like(blank)
        for g in range(KVH):
            blank_copy(g).start()

    def step(t, carry):
        @pl.when(t < KVH)
        def _():
            backward(t)

        @pl.when(t >= KVH)
        def _():
            forwards(t - KVH)

        for k in range(2 * KVH):
            @pl.when(t == k)
            def _():
                run(k + 1)

        return carry

    lax.fori_loop(0, 2 * KVH, step, 0)

    for parity in range(2):
        @pl.when(y_hi == parity)
        def _():
            for g in range(KVH):
                sums = received(g, parity, 0, own[g])
                total[:, :, g * HEAD:(g + 1) * HEAD] = sums.astype(jnp.bfloat16)

    stores = [
        pltpu.make_async_copy(total.at[0], dk_out, out_sem.at[2 * KVH]),
        pltpu.make_async_copy(total.at[1], dv_out, out_sem.at[2 * KVH + 1]),
    ]
    for store in stores:
        store.start()
    for g in range(KVH):
        grad_copy(g).wait()
        for r in range(1, SLOTS_SEEN):
            term(g, 0, r).wait_send()
    for parity in range(2):
        @pl.when(y_hi == parity)
        def _():
            for unit in UNITS:
                for slot in range(SLOTS_SEEN):
                    for p, r, way in fed(TREES[unit[3]], parity, slot):
                        message(unit, p, r, way).wait_send()

    @pl.when(pipe < pipes - 1)
    def _():
        for g in range(KVH):
            hand(g).wait_send()

    @pl.when(pipe > 0)
    def _():
        for g in range(KVH):
            hand(g).wait_recv()

    @pl.when(pipe == 0)
    def _():
        for g in range(KVH):
            blank_copy(g).wait()

    for store in stores:
        store.wait()


def settle(*refs):
    ins, outs, held, sems = refs[:4], refs[4:8], refs[8:12], refs[12]
    fetched = [pltpu.make_async_copy(ins[i], held[i], sems.at[0, i]) for i in range(4)]
    stored = [pltpu.make_async_copy(held[i], outs[i], sems.at[1, i]) for i in range(4)]
    for copy in fetched:
        copy.start()
    for fetch, store in zip(fetched, stored):
        fetch.wait()
        store.start()
    for copy in stored:
        copy.wait()


def local(order, *arrays):
    bf16 = jnp.bfloat16
    wide, narrow = (TOK, KVH * WIDE), (TOK, KVH * HEAD)
    anywhere = pl.BlockSpec(memory_space=pl.ANY)
    in_hbm = pl.BlockSpec(memory_space=pltpu.HBM)
    dma = pltpu.SemaphoreType.DMA
    outs = pl.pallas_call(
        kernel,
        out_shape=[jax.ShapeDtypeStruct(s, bf16) for s in (wide, wide, narrow, narrow)],
        in_specs=[pl.BlockSpec(memory_space=pltpu.SMEM)] + [in_hbm] * 7,
        out_specs=[anywhere] * 4,
        scratch_shapes=[
            pltpu.VMEM((SLOTS_SEEN, KVH, 2, TOK, HEAD), bf16),
            pltpu.VMEM((SLOTS_SEEN, KVH, 2, TOK, HEAD), bf16),
            pltpu.VMEM(wide, bf16),
            pltpu.VMEM(wide, bf16),
            pltpu.VMEM(wide, bf16),
            pltpu.VMEM(wide, bf16),
            pltpu.VMEM(wide, bf16),
            pltpu.VMEM((KVH, SLOTS_SEEN, 2, TOK, HEAD), bf16),
            pltpu.VMEM((KVH, 2, TOK, HEAD), jnp.float32),
            pltpu.VMEM((KVH, 2, SLOTS_SEEN, 2, TOK, HEAD), bf16),
            pltpu.VMEM((2,) + narrow, bf16),
            pltpu.VMEM((TOK, WIDE), bf16),
            dma((3,)),
            dma((2, KVH, 2)),
            dma((2 * KVH + 2,)),
            dma((2, KVH, 2, SLOTS_SEEN)),
            dma((2, KVH, SLOTS_SEEN)),
            dma((KVH, SLOTS_SEEN)),
            dma((KVH, 2, SLOTS_SEEN)),
            dma((KVH,)),
            dma((KVH,)),
        ],
        compiler_params=pltpu.CompilerParams(
            collective_id=0, has_side_effects=True, vmem_limit_bytes=VMEM_BYTES
        ),
    )(order, *[a[0] for a in arrays])
    outs = pl.pallas_call(
        settle,
        out_shape=[jax.ShapeDtypeStruct(out.shape, out.dtype) for out in outs],
        in_specs=[in_hbm] * 4,
        out_specs=[in_hbm] * 4,
        scratch_shapes=[pltpu.VMEM(out.shape, out.dtype) for out in outs] + [dma((2, 4))],
        compiler_params=pltpu.CompilerParams(vmem_limit_bytes=VMEM_BYTES),
    )(*outs)
    return tuple(out[None] for out in outs)


def solution(mesh):
    split = P("pipe", ("blk", "uly"), None)
    return jax.shard_map(
        local,
        mesh=mesh,
        in_specs=(P(),) + (split,) * 7,
        out_specs=(split,) * 4,
        check_vma=False,
    )
```

```python
import functools
import functools
import math

import jax
import jax.numpy as jnp
from jax import lax
from jax.experimental import pallas as pl
from jax.experimental.pallas import tpu as pltpu
from jax.sharding import PartitionSpec as P

HEAD = 128
GQA = 8
KVH = 4
TOK = 64
SLOTS_SEEN = 8
KEYS = SLOTS_SEEN * TOK
ROWS = GQA * TOK
WIDE = GQA * HEAD
NEG = -1e30
SCALE = HEAD ** -0.5
SCALE2 = SCALE * math.log2(math.e)
VMEM_BYTES = 60 * 1024 * 1024
TREES = (
    (
        {1: (0, 0, "P"), 2: (0, 0, "U"), 3: (1, 2, "X"), 4: (0, 2, "P"), 5: (1, 2, "D"), 6: (0, 3, "U"), 7: (0, 5, "U")},
        {1: (1, 0, "P"), 2: (1, 0, "U"), 3: (0, 0, "X"), 4: (1, 3, "P"), 5: (0, 2, "X"), 6: (1, 1, "U"), 7: (0, 1, "ZX")},
    ),
    (
        {1: (0, 0, "P"), 2: (0, 0, "U"), 3: (1, 2, "X"), 4: (0, 2, "P"), 5: (1, 1, "ZX"), 6: (0, 3, "U"), 7: (0, 5, "U")},
        {1: (1, 0, "P"), 2: (1, 0, "U"), 3: (0, 0, "X"), 4: (1, 3, "P"), 5: (1, 3, "U"), 6: (1, 1, "U"), 7: (1, 4, "U")},
    ),
    (
        {1: (0, 0, "P"), 2: (0, 0, "U"), 3: (1, 0, "ZX"), 4: (0, 2, "P"), 5: (1, 2, "D"), 6: (1, 2, "ZX"), 7: (0, 3, "ZP")},
        {1: (1, 0, "P"), 2: (1, 0, "U"), 3: (0, 0, "X"), 4: (1, 3, "P"), 5: (0, 2, "X"), 6: (1, 1, "U"), 7: (0, 1, "ZX")},
    ),
)
UNITS = ((0, 0, 1, 0), (0, 1, 1, 0), (0, 2, 1, 0), (0, 3, 1, 0), (1, 0, 2, 1), (1, 2, 2, 1))
BACK = (2, 2, 2, 2)
WAYS = tuple(sorted({way for tree in TREES for slots in tree for _, _, way in slots.values()}))


def fed(tree, parity, slot):
    found = [
        (p, r, way) for p in range(2) for r, (q, source, way) in tree[p].items() if (q, source) == (parity, slot)
    ]
    return sorted(found, key=lambda f: -chain(tree, f[0], f[1]))


def chain(tree, parity, slot):
    return 1 + max([chain(tree, p, r) for p, r, _ in fed(tree, parity, slot)], default=0)


EVEN = (
    (("fwd", 0, 3), ("fwd", 0, 0), ("fwd", 0, 1), ("fwd", 0, 4), ("fwd", 0, 2), ("fwd", 2, 0), ("fwd", 1, 0),
     ("fwd", 0, 5), ("fwd", 1, 1), ("fwd", 2, 4), ("fwd", 3, 0), ("fwd", 2, 2), ("fwd", 5, 0), ("fwd", 2, 1),
     ("fwd", 1, 2), ("fwd", 2, 3), ("fwd", 3, 1), ("fwd", 5, 1), ("fwd", 3, 2), ("fwd", 2, 5), ("fwd", 1, 3),
     ("last", 0, 0),),
    (("fwd", 5, 2), ("fwd", 5, 4), ("ret", 4, 0), ("ret", 7, 0), ("ret", 5, 0), ("ret", 6, 0), ("last", 0, 1),
     ("fwd", 3, 3), ("fwd", 5, 3),),
    (("fwd", 3, 4), ("ret", 7, 1), ("ret", 6, 1), ("ret", 5, 1), ("ret", 4, 1), ("last", 0, 2),),
    (("fwd", 5, 5), ("ret", 3, 0), ("ret", 7, 2), ("fwd", 3, 5), ("ret", 5, 2), ("ret", 6, 2), ("last", 0, 3),),
    (("ret", 7, 3), ("ret", 5, 3), ("ret", 4, 3), ("ret", 6, 3), ("ret", 3, 1), ("last", 0, 4), ("ret", 4, 2),),
    (),
    (("ret", 2, 0), ("ret", 2, 1), ("ret", 1, 0), ("ret", 1, 1), ("last", 0, 5), ("ret", 3, 2),),
    (("ret", 1, 3), ("ret", 1, 2), ("ret", 3, 3),),
    (("ret", 2, 2), ("ret", 2, 3),),
)
ODD = (
    (("fwd", 0, 0), ("fwd", 0, 1), ("fwd", 0, 2), ("fwd", 0, 4), ("fwd", 2, 0), ("fwd", 1, 0), ("fwd", 0, 3),
     ("fwd", 2, 1), ("fwd", 2, 2), ("fwd", 1, 1), ("fwd", 1, 2), ("fwd", 3, 0), ("fwd", 0, 5), ("fwd", 1, 4),
     ("fwd", 1, 3), ("fwd", 3, 1), ("fwd", 2, 3), ("fwd", 3, 2), ("fwd", 2, 4), ("last", 0, 0), ("fwd", 1, 5),
     ("fwd", 3, 4),),
    (("fwd", 2, 5), ("fwd", 3, 3), ("fwd", 3, 5), ("last", 0, 1),),
    (("ret", 5, 1), ("last", 0, 2), ("ret", 7, 0),),
    (("ret", 6, 1), ("ret", 7, 1), ("fwd", 4, 4), ("last", 0, 3), ("ret", 5, 0), ("ret", 5, 2), ("ret", 4, 0),
     ("ret", 6, 0),),
    (("ret", 7, 3), ("ret", 6, 2), ("ret", 4, 3), ("ret", 4, 2), ("fwd", 4, 5), ("ret", 5, 3), ("ret", 7, 2),
     ("ret", 4, 1), ("ret", 3, 0), ("last", 0, 4),),
    (("ret", 2, 0), ("ret", 3, 3),),
    (("ret", 6, 3), ("ret", 1, 2), ("last", 0, 5),),
    (("ret", 3, 1), ("ret", 1, 1), ("ret", 2, 1), ("ret", 3, 2),),
    (("ret", 1, 0), ("ret", 2, 3), ("ret", 1, 3), ("ret", 2, 2),),
)
MESH = pl.DeviceIdType.MESH

NT = (((1,), (1,)), ((), ()))
NN = (((1,), (0,)), ((), ()))
TN = (((0,), (0,)), ((), ()))


def dot(a, b, dims):
    return lax.dot_general(a, b, dims, preferred_element_type=jnp.float32)


def kernel(
    order, qf_in, kf_in, vf_in, qb_in, kb_in, vb_in, do_in,
    handed_out, dq_out, dk_out, dv_out,
    kvf, kvb, qf, qb, do, att, dq, part, own, got, total, blank,
    in_sem, kv_sem, out_sem, g_send, g_recv, r_send, r_recv, h_send, h_recv,
):
    pipe, pipes = lax.axis_index("pipe"), lax.axis_size("pipe")
    blk, blks = lax.axis_index("blk"), lax.axis_size("blk")
    uly = lax.axis_index("uly")
    y_hi = lax.rem(blk, 2)
    z, planes = blk // 2, blks // 2

    partner = {"uly": 1 - uly}
    flip = blk + 1 - 2 * y_hi

    def ring(group):
        return lax.rem(group + 2 * blks, blks)

    up = {
        "P": partner,
        "X": {"blk": flip, "uly": 1 - uly},
        "D": {"blk": flip},
        "U": {"blk": ring(blk + 2)},
        "ZP": {"blk": ring(blk + 2), "uly": 1 - uly},
        "ZX": {"blk": ring(flip + 2), "uly": 1 - uly},
        "ZZX": {"blk": ring(flip + 4), "uly": 1 - uly},
    }
    down = dict(
        up,
        U={"blk": ring(blk - 2)},
        ZP={"blk": ring(blk - 2), "uly": 1 - uly},
        ZX={"blk": ring(flip - 2), "uly": 1 - uly},
        ZZX={"blk": ring(flip - 4), "uly": 1 - uly},
    )
    after = {"pipe": lax.rem(pipe + 1, pipes)}
    before = {"pipe": lax.rem(pipe + pipes - 1, pipes)}

    barrier = pltpu.get_barrier_semaphore()
    peers = [up[way] for way in WAYS] + [down[way] for way in WAYS if way not in "PXD"] + [after, before]
    for peer in peers:
        pl.semaphore_signal(barrier, inc=1, device_id=peer, device_id_type=MESH)

    kv_loads = {}
    for phase, sources in enumerate(((kb_in, vb_in), (kf_in, vf_in))):
        for g in range(KVH):
            kv_loads[phase, g] = [
                pltpu.make_async_copy(
                    source.at[:, g * HEAD:(g + 1) * HEAD], (kvb, kvf)[phase].at[0, g, c], kv_sem.at[phase, g, c]
                )
                for c, source in enumerate(sources)
            ]
    loads = [
        pltpu.make_async_copy(qb_in, qb, in_sem.at[0]),
        pltpu.make_async_copy(do_in, do, in_sem.at[1]),
        pltpu.make_async_copy(qf_in, qf, in_sem.at[2]),
    ]
    for pair in kv_loads.values():
        for load in pair:
            load.start()
    for load in loads:
        load.start()

    def message(unit, parity, r, way, source=0):
        phase, head, count, _ = unit
        kv = (kvb, kvf)[phase]
        return pltpu.make_async_remote_copy(
            src_ref=kv.at[source, pl.ds(head, count)],
            dst_ref=kv.at[r, pl.ds(head, count)],
            send_sem=g_send.at[phase, head, parity, r],
            recv_sem=g_recv.at[phase, head, r],
            device_id=up[way],
            device_id_type=MESH,
        )

    def arrived(unit, r):
        message(unit, 0, r, "P").wait_recv()

    def send_on(unit, parity, slot):
        phase, head, count, tree = unit
        if slot:
            arrived(unit, slot)
        else:
            for g in range(head, head + count):
                for load in kv_loads[phase, g]:
                    load.wait()
        for p, r, way in fed(TREES[tree], parity, slot):
            message(unit, p, r, way, slot).start()

    def wait_others(unit, parity, _):
        for r in range(1, SLOTS_SEEN):
            if not fed(TREES[unit[3]], parity, r):
                arrived(unit, r)

    def term(g, parity, r):
        return pltpu.make_async_remote_copy(
            src_ref=part.at[g, r],
            dst_ref=got.at[g, parity, r],
            send_sem=r_send.at[g, r],
            recv_sem=r_recv.at[g, parity, r],
            device_id=down[TREES[BACK[g]][parity][r][2]],
            device_id_type=MESH,
        )

    def received(g, parity, slot, sums):
        for p, r, _ in reversed(fed(TREES[BACK[g]], parity, slot)):
            term(g, p, r).wait_recv()
            sums = sums + got[g, p, r].astype(jnp.float32)
        return sums

    def send_back(g, parity, slot):
        if fed(TREES[BACK[g]], parity, slot):
            sums = received(g, parity, slot, part[g, slot].astype(jnp.float32))
            part[g, slot] = sums.astype(jnp.bfloat16)
        term(g, parity, slot).start()

    def run(k):
        for parity, table in enumerate((EVEN, ODD)):
            @pl.when(y_hi == parity)
            def _():
                for name, slot, index in table[k]:
                    if name == "ret":
                        send_back(index, parity, slot)
                    else:
                        {"fwd": send_on, "last": wait_others}[name](UNITS[index], parity, slot)

    y = 2 * y_hi + uly
    col_p, col_x, col_d = 2 * y_hi + 1 - uly, 3 - y, 2 * (1 - y_hi) + uly
    plane = [4 * lax.rem(z + planes - k, planes) for k in range(3)]
    o = 1 - y_hi
    held = [
        plane[0] + y,
        plane[0] + col_p,
        plane[1] + y,
        o * plane[1] + y_hi * plane[0] + col_x,
        o * (plane[1] + col_p) + y_hi * (plane[0] + col_d),
        plane[1] + o * col_d + y_hi * col_x,
        o * (plane[2] + col_x) + y_hi * (plane[1] + col_p),
        o * plane[2] + y_hi * plane[1] + col_d,
    ]
    mine = order[held[0]]
    offsets = [0.0] + [jnp.where(order[held[r]] < mine, 0.0, NEG) for r in range(1, SLOTS_SEEN)]

    def stacked(ref, g):
        return jnp.concatenate(
            [ref[:, pl.ds(pl.multiple_of(g * WIDE + h * HEAD, HEAD), HEAD)] for h in range(GQA)], axis=0
        )

    def keys(ref, c, g):
        return ref[:, g, c].reshape(KEYS, HEAD)

    def raised(k, q):
        raw = dot(k, q, NT)
        key = lax.broadcasted_iota(jnp.int32, (TOK, q.shape[0]), 0)
        row = lax.broadcasted_iota(jnp.int32, (TOK, q.shape[0]), 1) % TOK
        blocks = [jnp.where(key <= row, raw[:TOK], NEG)]
        blocks += [raw[r * TOK:(r + 1) * TOK] for r in range(1, SLOTS_SEEN)]
        peaks = [jnp.max(block, axis=0, keepdims=True) + offset for block, offset in zip(blocks, offsets)]
        peak = functools.reduce(jnp.maximum, peaks)
        p = jnp.concatenate(
            [jnp.exp2((block - (peak - offset)) * SCALE2) for block, offset in zip(blocks, offsets)], axis=0
        )
        return p, 1.0 / jnp.sum(p, axis=0, keepdims=True)

    def spread(ref, g, value):
        for h in range(GQA):
            ref[:, pl.ds(pl.multiple_of(g * WIDE + h * HEAD, HEAD), HEAD)] = value[h * TOK:(h + 1) * TOK]

    def columns(ref, g):
        return ref.at[:, pl.ds(pl.multiple_of(g * WIDE, WIDE), WIDE)]

    def grad_copy(g):
        return pltpu.make_async_copy(columns(dq, g), columns(dq_out, g), out_sem.at[g])

    def blank_copy(g):
        return pltpu.make_async_copy(blank, columns(handed_out, g), out_sem.at[KVH + g])

    def hand(g):
        return pltpu.make_async_remote_copy(
            src_ref=columns(att, g),
            dst_ref=columns(handed_out, g),
            send_sem=h_send.at[g],
            recv_sem=h_recv.at[g],
            device_id=after,
            device_id_type=MESH,
        )

    def backward(g):
        k, v = keys(kvb, 0, g), keys(kvb, 1, g)
        q, up = stacked(qb, g), stacked(do, g)
        p, inverse = raised(k, q)
        p = p * inverse
        dp = dot(v, up, NT)
        delta = jnp.sum(p * dp, axis=0, keepdims=True)
        ds = (p * (dp - delta)).astype(jnp.bfloat16)
        dv = dot(p.astype(jnp.bfloat16), up, NN)
        dk = dot(ds, q, NN) * SCALE
        own[g, 0] = dk[:TOK]
        own[g, 1] = dv[:TOK]
        part[g, :, 0] = dk.reshape(SLOTS_SEEN, TOK, HEAD).astype(jnp.bfloat16)
        part[g, :, 1] = dv.reshape(SLOTS_SEEN, TOK, HEAD).astype(jnp.bfloat16)
        grad = dot(k, ds, TN) * SCALE
        spread(dq, g, grad.T.astype(jnp.bfloat16))
        grad_copy(g).start()

    def forwards(g):
        k, v = keys(kvf, 0, g), keys(kvf, 1, g)
        p, inverse = raised(k, stacked(qf, g))
        weighted = dot(v, p.astype(jnp.bfloat16), TN) * inverse
        spread(att, g, weighted.T.astype(jnp.bfloat16))

        @pl.when(pipe < pipes - 1)
        def _():
            hand(g).start()

    pl.semaphore_wait(barrier, len(peers))
    run(0)
    for load in loads:
        load.wait()

    @pl.when(pipe == 0)
    def _():
        blank[...] = jnp.zeros_like(blank)
        for g in range(KVH):
            blank_copy(g).start()

    def step(t, carry):
        @pl.when(t < KVH)
        def _():
            backward(t)

        @pl.when(t >= KVH)
        def _():
            forwards(t - KVH)

        for k in range(2 * KVH):
            @pl.when(t == k)
            def _():
                run(k + 1)

        return carry

    lax.fori_loop(0, 2 * KVH, step, 0)

    for parity in range(2):
        @pl.when(y_hi == parity)
        def _():
            for g in range(KVH):
                sums = received(g, parity, 0, own[g])
                total[:, :, g * HEAD:(g + 1) * HEAD] = sums.astype(jnp.bfloat16)

    stores = [
        pltpu.make_async_copy(total.at[0], dk_out, out_sem.at[2 * KVH]),
        pltpu.make_async_copy(total.at[1], dv_out, out_sem.at[2 * KVH + 1]),
    ]
    for store in stores:
        store.start()
    for g in range(KVH):
        grad_copy(g).wait()
        for r in range(1, SLOTS_SEEN):
            term(g, 0, r).wait_send()
    for parity in range(2):
        @pl.when(y_hi == parity)
        def _():
            for unit in UNITS:
                for slot in range(SLOTS_SEEN):
                    for p, r, way in fed(TREES[unit[3]], parity, slot):
                        message(unit, p, r, way).wait_send()

    @pl.when(pipe < pipes - 1)
    def _():
        for g in range(KVH):
            hand(g).wait_send()

    @pl.when(pipe > 0)
    def _():
        for g in range(KVH):
            hand(g).wait_recv()

    @pl.when(pipe == 0)
    def _():
        for g in range(KVH):
            blank_copy(g).wait()

    for store in stores:
        store.wait()


def settle(*refs):
    ins, outs, held, sems = refs[:4], refs[4:8], refs[8:12], refs[12]
    moves = []
    for i, pieces in enumerate((4, 4, 1, 1)):
        rows = TOK // pieces
        for piece in range(pieces):
            here, slot = pl.ds(piece * rows, rows), len(moves)
            moves.append((
                pltpu.make_async_copy(ins[i].at[here], held[i].at[here], sems.at[0, slot]),
                pltpu.make_async_copy(held[i].at[here], outs[i].at[here], sems.at[1, slot]),
            ))
    for fetch, _ in moves:
        fetch.start()
    for fetch, store in moves:
        fetch.wait()
        store.start()
    for _, store in moves:
        store.wait()


def local(order, *arrays):
    bf16 = jnp.bfloat16
    wide, narrow = (TOK, KVH * WIDE), (TOK, KVH * HEAD)
    anywhere = pl.BlockSpec(memory_space=pl.ANY)
    in_hbm = pl.BlockSpec(memory_space=pltpu.HBM)
    dma = pltpu.SemaphoreType.DMA
    outs = pl.pallas_call(
        kernel,
        out_shape=[jax.ShapeDtypeStruct(s, bf16) for s in (wide, wide, narrow, narrow)],
        in_specs=[pl.BlockSpec(memory_space=pltpu.SMEM)] + [in_hbm] * 7,
        out_specs=[anywhere] * 4,
        scratch_shapes=[
            pltpu.VMEM((SLOTS_SEEN, KVH, 2, TOK, HEAD), bf16),
            pltpu.VMEM((SLOTS_SEEN, KVH, 2, TOK, HEAD), bf16),
            pltpu.VMEM(wide, bf16),
            pltpu.VMEM(wide, bf16),
            pltpu.VMEM(wide, bf16),
            pltpu.VMEM(wide, bf16),
            pltpu.VMEM(wide, bf16),
            pltpu.VMEM((KVH, SLOTS_SEEN, 2, TOK, HEAD), bf16),
            pltpu.VMEM((KVH, 2, TOK, HEAD), jnp.float32),
            pltpu.VMEM((KVH, 2, SLOTS_SEEN, 2, TOK, HEAD), bf16),
            pltpu.VMEM((2,) + narrow, bf16),
            pltpu.VMEM((TOK, WIDE), bf16),
            dma((3,)),
            dma((2, KVH, 2)),
            dma((2 * KVH + 2,)),
            dma((2, KVH, 2, SLOTS_SEEN)),
            dma((2, KVH, SLOTS_SEEN)),
            dma((KVH, SLOTS_SEEN)),
            dma((KVH, 2, SLOTS_SEEN)),
            dma((KVH,)),
            dma((KVH,)),
        ],
        compiler_params=pltpu.CompilerParams(
            collective_id=0, has_side_effects=True, vmem_limit_bytes=VMEM_BYTES
        ),
    )(order, *[a[0] for a in arrays])
    outs = pl.pallas_call(
        settle,
        out_shape=[jax.ShapeDtypeStruct(out.shape, out.dtype) for out in outs],
        in_specs=[in_hbm] * 4,
        out_specs=[in_hbm] * 4,
        scratch_shapes=[pltpu.VMEM(out.shape, out.dtype) for out in outs] + [dma((2, 10))],
        compiler_params=pltpu.CompilerParams(vmem_limit_bytes=VMEM_BYTES),
    )(*outs)
    return tuple(out[None] for out in outs)


def solution(mesh):
    split = P("pipe", ("blk", "uly"), None)
    return jax.shard_map(
        local,
        mesh=mesh,
        in_specs=(P(),) + (split,) * 7,
        out_specs=(split,) * 4,
        check_vma=False,
    )
```
